1024 devices in a mesh: dp: 16 (over z), group: 8 (over y), inner: 8 (over x, core).
Axes of the slice: x: 4, y: 8, z: 16, core: 2. Of those that a mesh axis runs over, the one named last changes fastest.
Arguments:
- token_inputs: bfloat16 [1024, 3584], P(('group', 'inner')), may hold values from -1 to 1
- out_grads: bfloat16 [1024, 3584], P(('group', 'inner')), may hold values from -2 to 2
- expert_ids: int32 [1024, 8], P(('group', 'inner')), may hold values from 0 to 127, as said below
- router_weight: float32 [3584, 128], replicated, may hold values from -1.6 to 1.6
- gate_weight: bfloat16 [128, 3584, 1024], P(('group', 'inner'), None, 'dp'), may hold values from -0.09375 to 0.09375
- up_weight: bfloat16 [128, 3584, 1024], P(('group', 'inner'), None, 'dp'), may hold values from -0.09375 to 0.09375
- down_weight: bfloat16 [128, 1024, 3584], P(('group', 'inner'), 'dp'), may hold values from -0.1875 to 0.1875
- saved_gate: bfloat16 [128, 128, 1024], P(('group', 'inner'), None, 'dp'), may hold values from -6 to 6
- saved_up: bfloat16 [128, 128, 1024], P(('group', 'inner'), None, 'dp'), may hold values from -6 to 6
Outputs:
- input_grad: bfloat16 [1024, 3584], P(('group', 'inner'), 'dp')
- router_grad: float32 [3584, 128], P('dp')
The draws below stay inside these ranges and needn't reach their ends.
Inputs may be any that keep to these rules, and one draw needn't show every extreme that they name: `expert_ids`: each token names 8 different experts, 2 in each of 4 node groups, expert e lying in node group e // 16. One node group is among those of every token. Among the 16 tokens of one block (the rows of one device) no expert is named more than 2 times, and in every block some experts are named exactly 2 times.
All inputs are finite; a program needn't handle non-finite values.
Results may differ from the reference program's by a relative error of at most 0.014.
Values may be sent and summed in bfloat16 or wider, within the bound.
A program may use at most 32 MiB of HBM per device.

```python
import jax
import jax.numpy as jnp
from jax import lax

D = 3584
FF = 1024
TOPK = 8
TOK_DEV = 16
EXPERTS = 128
EXP_GROUP = 16
TOPG = 4
PER_GROUP = 2
CAP = 2
SLOTS = 128
TOKENS = 1024
N_DP = 16


def draw_expert_ids(key, part):
    key = jax.random.fold_in(key, 7)
    key_hot, key_pop, key_noise, key_perm = jax.random.split(key, 4)
    group_count = EXPERTS // EXP_GROUP
    block_count = TOKENS // TOK_DEV
    labels = jnp.arange(group_count, dtype=jnp.int32)
    hot_group = jax.random.randint(key_hot, (), 0, group_count)
    popular = jax.random.randint(key_pop, (group_count,), 0, 4096)
    noise = jax.random.randint(key_noise, (TOKENS, group_count), 0, 4096)
    group_scores = (popular[None, :] + noise) * group_count + labels[None, :]
    group_scores = jnp.where(labels[None, :] == hot_group, 1 << 26, group_scores)
    unused, picked = lax.top_k(group_scores, TOPG)
    member = jnp.sum((picked[:, :, None] == labels[None, None, :]).astype(jnp.int32), axis=1)
    member = member.reshape(block_count, TOK_DEV, group_count)
    ranking = (jnp.cumsum(member, axis=1) - member).reshape(TOKENS, group_count)
    rank_of = jnp.take_along_axis(ranking, picked, axis=1)
    order_keys = jax.random.randint(key_perm, (block_count, group_count, EXP_GROUP), 0, 1 << 20) * EXP_GROUP + jnp.arange(EXP_GROUP, dtype=jnp.int32)
    orders = jnp.argsort(order_keys, axis=2).astype(jnp.int32)
    block_of = jnp.arange(TOKENS, dtype=jnp.int32) // TOK_DEV
    offsets = (rank_of[:, :, None] * PER_GROUP + jnp.arange(PER_GROUP, dtype=jnp.int32)[None, None, :]) % EXP_GROUP
    local_ids = orders[block_of[:, None, None], picked[:, :, None], offsets]
    expert_list = picked[:, :, None] * EXP_GROUP + local_ids
    return expert_list.reshape(TOKENS, TOPK).astype(jnp.int32)


def block_scale(rng, extent, pieces, least, high):
    gain = 1.0
    for dim, shards_of in pieces:
        heights = jax.random.uniform(jax.random.fold_in(jax.random.fold_in(rng, 6), dim), (shards_of,), jnp.float32, least / len(pieces), high / len(pieces))
        gain = gain * jnp.repeat(jnp.exp(heights), extent[dim] // shards_of).reshape((-1,) + (1,) * (len(extent) - 1 - dim))
    return gain


def bell_draw(stream_key, extent, deviation, bound, pieces=(), held_as=jnp.bfloat16):
    result = deviation * jax.random.normal(stream_key, extent, jnp.float32)
    if pieces:
        result = result * block_scale(stream_key, extent, pieces, -0.22, 0.18)
    return jnp.clip(result, -bound, bound).astype(held_as)


def setup_inputs(seed: int = 0) -> dict:
    splits = jax.random.split(jax.random.key(seed), 10)
    token_inputs = bell_draw(splits[0], (TOKENS, D), 0.125, 1.0, ((0, 64),))
    out_grads = bell_draw(splits[1], (TOKENS, D), 0.25, 2.0, ((0, 64),))
    expert_ids = draw_expert_ids(jax.random.fold_in(splits[9], 71), 0)
    router_weight = bell_draw(splits[3], (D, EXPERTS), 0.2, 1.6, (), jnp.float32)
    gate_weight = bell_draw(splits[4], (EXPERTS, D, FF), D ** -0.5, 0.09375, ((0, 64), (2, 16)))
    up_weight = bell_draw(splits[5], (EXPERTS, D, FF), D ** -0.5, 0.09375, ((0, 64), (2, 16)))
    down_weight = bell_draw(splits[6], (EXPERTS, FF, D), FF ** -0.5, 0.1875, ((0, 64), (1, 16)))
    saved_gate = bell_draw(splits[7], (EXPERTS, SLOTS, FF), 1.0, 6.0, ((0, 64), (2, 16)))
    saved_up = bell_draw(splits[8], (EXPERTS, SLOTS, FF), 1.0, 6.0, ((0, 64), (2, 16)))
    return {"token_inputs": token_inputs, "out_grads": out_grads, "expert_ids": expert_ids, "router_weight": router_weight, "gate_weight": gate_weight, "up_weight": up_weight, "down_weight": down_weight, "saved_gate": saved_gate, "saved_up": saved_up}


route_scale = 2.5


def expert_grads(operands):
    rows, gate_w, up_w, down_w, saved_g, saved_u = operands
    block_width = FF // N_DP
    hidden_grad = jnp.dot(rows, down_w.T, preferred_element_type=jnp.float32)
    pre_gate = saved_g.astype(jnp.float32)
    pre_up = saved_u.astype(jnp.float32)
    sigmoid_gate = jax.nn.sigmoid(pre_gate)
    swish_gate = pre_gate * sigmoid_gate
    gate_blocks = jnp.sum((swish_gate * pre_up * hidden_grad).reshape(SLOTS, N_DP, block_width), axis=2)
    gate_blocks = lax.optimization_barrier(gate_blocks.astype(jnp.bfloat16)).astype(jnp.float32)
    gate_total = jnp.sum(gate_blocks, axis=1)
    d_gate = (hidden_grad * pre_up * sigmoid_gate * (1.0 + pre_gate * (1.0 - sigmoid_gate))).astype(jnp.bfloat16)
    d_up = (hidden_grad * swish_gate).astype(jnp.bfloat16)
    d_gate = lax.optimization_barrier(d_gate).astype(jnp.float32).reshape(SLOTS, N_DP, block_width)
    d_up = lax.optimization_barrier(d_up).astype(jnp.float32).reshape(SLOTS, N_DP, block_width)
    gate_mat = gate_w.astype(jnp.float32).reshape(D, N_DP, block_width)
    up_mat = up_w.astype(jnp.float32).reshape(D, N_DP, block_width)
    row_parts = jnp.einsum('snf,dnf->nsd', d_gate, gate_mat) + jnp.einsum('snf,dnf->nsd', d_up, up_mat)
    row_parts = lax.optimization_barrier(row_parts.astype(jnp.bfloat16)).astype(jnp.float32)
    return jnp.sum(row_parts, axis=0), gate_total


def reference(token_inputs, out_grads, expert_ids, router_weight, gate_weight, up_weight, down_weight, saved_gate, saved_up):
    block_count = TOKENS // TOK_DEV
    scores = jnp.dot(token_inputs.astype(jnp.float32), router_weight, precision=lax.Precision.HIGHEST)
    affinity = jax.nn.sigmoid(scores)
    chosen = jnp.take_along_axis(affinity, expert_ids, axis=1)
    affinity_sum = jnp.sum(chosen, axis=1, keepdims=True)
    mixing = route_scale * chosen / affinity_sum
    blocks = expert_ids.reshape(block_count, TOK_DEV, TOPK)
    onehot = (blocks[..., None] == jnp.arange(EXPERTS, dtype=jnp.int32)).astype(jnp.int32)
    per_token = jnp.sum(onehot, axis=2)
    before = jnp.cumsum(per_token, axis=1) - per_token
    position = jnp.sum(onehot * before[:, :, None, :], axis=3)
    slot = (jnp.arange(block_count, dtype=jnp.int32)[:, None, None] * CAP + position).reshape(TOKENS, TOPK).astype(jnp.int32)
    token_rows = jnp.broadcast_to(jnp.arange(TOKENS, dtype=jnp.int32)[:, None], (TOKENS, TOPK))
    grad_buffer = jnp.zeros((EXPERTS, SLOTS, D), jnp.bfloat16).at[expert_ids, slot].set(out_grads[token_rows])
    row_sums, gate_sums = lax.map(expert_grads, (grad_buffer, gate_weight, up_weight, down_weight, saved_gate, saved_up))
    picked = row_sums[expert_ids, slot]
    expert_grad = jnp.sum(mixing[:, :, None] * picked, axis=1)
    gate_grad = gate_sums[expert_ids, slot]
    weighted = jnp.sum(gate_grad * chosen, axis=1, keepdims=True)
    slope = route_scale * (gate_grad / affinity_sum - weighted / (affinity_sum * affinity_sum)) * chosen * (1.0 - chosen)
    matches = (expert_ids[:, :, None] == jnp.arange(EXPERTS, dtype=jnp.int32)).astype(jnp.float32)
    logit_grad = jnp.sum(matches * slope[:, :, None], axis=1)
    input_grad = (expert_grad + jnp.dot(logit_grad, router_weight.T, precision=lax.Precision.HIGHEST)).astype(jnp.bfloat16)
    router_grad = jnp.dot(token_inputs.astype(jnp.float32).T, logit_grad, precision=lax.Precision.HIGHEST)
    return input_grad, router_grad
```

```python
import functools

import jax
import jax.numpy as jnp
from jax import lax
from jax.experimental import pallas as pl
from jax.experimental.pallas import tpu as pltpu
from jax.sharding import PartitionSpec as P

MESH = pl.DeviceIdType.MESH
route_scale = 2.5
f32, bf16 = jnp.float32, jnp.bfloat16
HI = lax.Precision.HIGHEST
CHUNKS = 2


def dot_nt(a, b, **kw):
    return lax.dot_general(a, b, (((1,), (1,)), ((), ())), preferred_element_type=f32, **kw)


def dot_nn(a, b):
    return lax.dot_general(a, b, (((1,), (0,)), ((), ())), preferred_element_type=f32)


def iota(shape, dim):
    return lax.broadcasted_iota(jnp.int32, shape, dim)


def kernel(
    NZ, NG, NI, K,
    pay1, pay2, scores, rw_hbm, gw_hbm, uw_hbm, dw_hbm, sg_hbm, su_hbm,
    out_x, out_r,
    gwv, uwv, dwv, sgv, suv, rwv,
    buf1, buf2, buf3, pt, pmix, wT, tokT, xt, dgu, gz, bufG, gflat, gt, lg,
    rs_src, rs_dst, finv, tbuf, rbuf, ysrc, yacc, ydst,
    load_sem, ys, yr, xs, xr, ag_s, ag_r, rs_s, rs_r, z_s, z_r,
):
    NB = NG * NI
    T = 16 * NB
    S = 2 * NB
    E = 2 * NB
    FP = pay1.shape[1]
    FS = rwv.shape[0]
    F = dwv.shape[1]
    D = dwv.shape[2]
    half = NZ // 2
    CR = FS // CHUNKS
    g, i, n = lax.axis_index("group"), lax.axis_index("inner"), lax.axis_index("dp")
    q = g * NI + i

    loads = [
        pltpu.make_async_copy(dw_hbm, dwv, load_sem.at[0]),
        pltpu.make_async_copy(sg_hbm, sgv, load_sem.at[1]),
        pltpu.make_async_copy(su_hbm, suv, load_sem.at[2]),
        pltpu.make_async_copy(gw_hbm, gwv, load_sem.at[3]),
        pltpu.make_async_copy(uw_hbm, uwv, load_sem.at[4]),
        pltpu.make_async_copy(
            rw_hbm.at[pl.ds(pl.multiple_of(n * FS, 8), FS)], rwv, load_sem.at[5]
        ),
    ]
    for c in loads:
        c.start()

    def each(count, fn):
        def body(r, carry):
            fn(r)
            return carry

        lax.fori_loop(1, count, body, 0)

    def peer(axis, r):
        me, size = {"group": (g, NG), "inner": (i, NI), "dp": (n, NZ)}[axis]
        return {axis: lax.rem(me + r, size)}

    bar = pltpu.get_barrier_semaphore()
    for axis, size in (("group", NG), ("inner", NI), ("dp", NZ)):
        each(
            size,
            lambda r, axis=axis: pl.semaphore_signal(
                bar, inc=1, device_id=peer(axis, r), device_id_type=MESH
            ),
        )
    pl.semaphore_wait(bar, NG + NI + NZ - 3)

    def remote(src, dst, s, r, dev):
        return pltpu.make_async_remote_copy(
            src_ref=src, dst_ref=dst, send_sem=s, recv_sem=r, device_id=dev, device_id_type=MESH
        )

    def y_copy(t, r):
        src, dst = ((pay1, buf1), (pay2, buf2), (scores, buf3))[t]
        return remote(src, dst.at[g, i], ys.at[t, r], yr.at[t, r], peer("group", r))

    def x_copy(t, r):
        buf = (buf1, buf2, buf3)[t]
        return remote(buf.at[:, i], buf.at[:, i], xs.at[t, r], xr.at[t, r], peer("inner", r))

    each(NG, lambda r: y_copy(0, r).start())
    buf1[g, i] = pay1[...]
    each(NG, lambda r: y_copy(0, r).wait_recv())
    each(NI, lambda r: x_copy(0, r).start())
    each(NG, lambda r: y_copy(1, r).start())
    each(NG, lambda r: y_copy(2, r).start())
    buf2[g, i] = pay2[...]
    buf3[g, i] = scores[...]
    each(NI, lambda r: x_copy(0, r).wait_recv())
    each(NG, lambda r: y_copy(1, r).wait_recv())
    each(NG, lambda r: y_copy(2, r).wait_recv())

    X = buf1[...].reshape(T, FP)
    sel = (iota((16, FP), 1) == iota((16, FP), 0) + FS).astype(bf16)
    codes = dot_nt(sel, X)
    srow = iota((S, T), 0)
    same = (srow >> 1) == (iota((S, T), 1) >> 4)
    for j in range(2):
        want = (2 * q + j + E * (iota((S, 1), 0) & 1)).astype(f32)
        hit = codes[0:1] == want
        for k in range(1, K):
            hit = hit | (codes[k : k + 1] == want)
        pt[pl.ds(j * S, S), :] = jnp.where(same & hit, 1.0, 0.0).astype(bf16)
    xs_rows = dot_nn(pt[...], X)
    xt[n] = xs_rows.T[0:FS].astype(bf16)

    def chunk(c):
        return pl.ds(c * CR, CR)

    def zdev(d):
        return {"dp": lax.rem(n + (1 if d == 0 else NZ - 1), NZ)}

    def ag_copy(d, st, c):
        m = lax.rem(n + (NZ - st if d == 0 else st), NZ)
        ref = xt.at[m, chunk(c)]
        return remote(ref, ref, ag_s.at[d, st, c], ag_r.at[d, st, c], zdev(d))

    def ag_has(d, st, c):
        return st < half - 1 or c == d or CHUNKS == 1

    def transpose_weights(part, parts):
        cols = D // parts
        for j in range(2):
            both = jnp.concatenate(
                (gwv[j, :, part * cols : (part + 1) * cols], uwv[j, :, part * cols : (part + 1) * cols]),
                axis=0,
            )
            wT[j, pl.ds(part * cols, cols), :] = both.astype(f32).T.astype(bf16)

    def fold_saved():
        for j in range(2):
            a = sgv[j].astype(f32)
            u = suv[j].astype(f32)
            sig = jax.nn.sigmoid(a)
            sw = a * sig
            dgu[j, 0] = u * sig * (1.0 + a * (1.0 - sig))
            dgu[j, 1] = sw

    def mix_tokens():
        codes_all = buf2[:, :, :, FP : FP + E].reshape(T, E).astype(f32)
        aff = jax.nn.sigmoid(buf3[...].reshape(T, E))
        named = jnp.where(codes_all > 0.0, aff, 0.0)
        mix = (route_scale * named / jnp.sum(named, axis=1, keepdims=True)).astype(bf16)
        owner = (iota((E, 2 * S), 1) >= S).astype(jnp.int32) + 2 * q
        pick = (iota((E, 2 * S), 0) == owner).astype(bf16)
        spread = dot_nn(mix, pick)
        placed = pt[...].astype(f32).T
        pmix[...] = (placed * spread).astype(bf16).reshape(NG, NI, 16, 2 * S)

    def token_transpose():
        tok = buf2[:, :, :, 0:FP].reshape(T, FP)
        tokT[...] = tok.astype(f32).T[0:FS].astype(bf16)

    parts = 7 if D % (7 * 128) == 0 else half
    for st in range(half):
        for c in range(CHUNKS):
            for d in range(2):
                if st > 0:
                    ag_copy(d, st - 1, c).wait_recv()
                if ag_has(d, st, c):
                    ag_copy(d, st, c).start()
        if st == 0:
            each(NI, lambda r: x_copy(1, r).start())
            each(NI, lambda r: x_copy(2, r).start())
            for c in loads:
                c.wait()
            fold_saved()
        if st == min(2, half - 1):
            each(NI, lambda r: x_copy(1, r).wait_recv())
            each(NI, lambda r: x_copy(2, r).wait_recv())
            mix_tokens()
        if st == min(3, half - 1):
            token_transpose()
        for p in range(parts):
            if p % half == st:
                transpose_weights(p, parts)
    for c in range(CHUNKS):
        for d in range(2):
            if ag_has(d, half - 1, c):
                ag_copy(d, half - 1, c).wait_recv()

    hid = dot_nn(dwv[...].reshape(2 * F, D), xt[...].reshape(D, 2 * S))
    both = []
    for j in range(2):
        h = hid[j * F : (j + 1) * F, j * S : (j + 1) * S]
        up = h * dgu[j, 1]
        gz[n, pl.ds(j, 1), :] = jnp.sum(up * suv[j].astype(f32), axis=0, keepdims=True)
        both.append(jnp.concatenate((h * dgu[j, 0], up), axis=0).astype(bf16))

    def z_copy(r):
        return remote(gz.at[n], gz.at[n], z_s.at[r], z_r.at[r], peer("dp", r))

    each(NZ, lambda r: z_copy(r).start())

    def part(m, c):
        rows = pl.ds(pl.multiple_of(m * FS + c * CR, 16), CR)
        return jnp.concatenate([dot_nn(wT[j, rows, :], both[j]) for j in range(2)], axis=1)

    def gx_copy(r):
        return remote(bufG.at[g, i], bufG.at[g, i], xs.at[3, r], xr.at[3, r], peer("inner", r))

    def gy_copy(r):
        return remote(bufG.at[g], bufG.at[g], ys.at[3, r], yr.at[3, r], peer("group", r))

    def router_side():
        for b in range(NB):
            gflat[2 * b : 2 * b + 2, :] = bufG[b // NI, b % NI]
        gt[...] = gflat[...].T

        def body(b, carry):
            gb, ib = b // NI, lax.rem(b, NI)
            code = buf2[gb, ib, :, FP : FP + E].astype(f32)
            aff = jax.nn.sigmoid(buf3[gb, ib])
            g0 = gt[pl.ds(2 * b, 1), :]
            g1 = gt[pl.ds(2 * b + 1, 1), :]
            grads = jnp.where(code == 1.0, g0, jnp.where(code == 2.0, g1, 0.0))
            named = jnp.where(code > 0.0, aff, 0.0)
            total = jnp.sum(named, axis=1, keepdims=True)
            weighted = jnp.sum(named * grads, axis=1, keepdims=True)
            lg[b] = route_scale * (grads / total - weighted / (total * total)) * named * (1.0 - aff)
            return carry

        lax.fori_loop(0, NB, body, 0)
        rest = lg[...].reshape(T, E)
        acc = None
        for _ in range(3):
            top = rest.astype(bf16)
            term = dot_nn(tokT[...], top)
            acc = term if acc is None else acc + term
            rest = rest - top.astype(f32)
        out_r[...] = acc

    def rs_copy(d, st, c):
        return remote(
            rs_src.at[d, st, chunk(c)], rs_dst.at[d, st, chunk(c)],
            rs_s.at[d, st, c], rs_r.at[d, st, c], zdev(d),
        )

    def rs_has(d, st, c):
        return st > 0 or c == d or CHUNKS == 1

    def rs_step(st, c, d):
        if not rs_has(d, st, c):
            return
        m = lax.rem(n + (half - st if d == 0 else NZ - half + st), NZ)
        acc = part(m, c)
        if st > 0 and rs_has(d, st - 1, c):
            rs_copy(d, st - 1, c).wait_recv()
            acc = acc + rs_dst[d, st - 1, chunk(c), :].astype(f32)
        rs_src[d, st, chunk(c), :] = acc.astype(bf16)
        rs_copy(d, st, c).start()

    for st in range(half):
        for c in range(CHUNKS):
            for d in range(2):
                rs_step(st, c if st else 1 - c, d)
        if st == min(1, half - 1):
            each(NZ, lambda r: z_copy(r).wait_recv())
            bufG[g, i] = jnp.sum(gz[...], axis=0)
            each(NI, lambda r: gx_copy(r).start())
        if st == min(3, half - 1):
            each(NI, lambda r: gx_copy(r).wait_recv())
            each(NG, lambda r: gy_copy(r).start())
        if st == min(5, half - 1):
            each(NG, lambda r: gy_copy(r).wait_recv())
            router_side()

    for c in range(CHUNKS):
        acc = part(n, c)
        for d in range(2):
            if rs_has(d, half - 1, c):
                rs_copy(d, half - 1, c).wait_recv()
                acc = acc + rs_dst[d, half - 1, chunk(c), :].astype(f32)
        finv[chunk(c), :] = acc.astype(bf16)
    if FP > FS:
        finv[FS:FP, :] = jnp.zeros((FP - FS, 2 * S), bf16)

    def tx_copy(r):
        return remote(tbuf.at[r], rbuf.at[r], xs.at[4, r], xr.at[4, r], peer("inner", r))

    def ty_copy(r):
        to = lax.rem(g + r, NG)
        return remote(ysrc.at[to], ydst.at[r], ys.at[4, r], yr.at[4, r], peer("group", r))

    def token_rows(at):
        return dot_nt(pmix[:, at].reshape(NG * 16, 2 * S), finv[...])

    def send_rows(r):
        tbuf[r] = token_rows(lax.rem(i + r, NI)).astype(bf16).reshape(NG, 16, FP)
        tx_copy(r).start()

    each(NI, send_rows)
    acc = token_rows(i)
    extra = dot_nt(lg[q], rwv[...], precision=HI)
    for r in range(1, NI):
        tx_copy(r).wait_recv()
        acc = acc + rbuf[r].astype(f32).reshape(NG * 16, FP)
    yacc[...] = acc.reshape(NG, 16, FP)
    ysrc[...] = acc.astype(bf16).reshape(NG, 16, FP)
    each(NG, lambda r: ty_copy(r).start())
    total = yacc[g]
    for r in range(1, NG):
        ty_copy(r).wait_recv()
        total = total + ydst[r].astype(f32)
    out_x[...] = (total[:, 0:FS] + extra).astype(bf16)

    for t in range(3):
        each(NG, lambda r, t=t: y_copy(t, r).wait_send())
        each(NI, lambda r, t=t: x_copy(t, r).wait_send())
    each(NZ, lambda r: z_copy(r).wait_send())
    each(NI, lambda r: gx_copy(r).wait_send())
    each(NG, lambda r: gy_copy(r).wait_send())
    each(NI, lambda r: tx_copy(r).wait_send())
    each(NG, lambda r: ty_copy(r).wait_send())
    for st in range(half):
        for c in range(CHUNKS):
            for d in range(2):
                if ag_has(d, st, c):
                    ag_copy(d, st, c).wait_send()
                if rs_has(d, st, c):
                    rs_copy(d, st, c).wait_send()


def local(
    token_inputs, out_grads, expert_ids, router_weight,
    gate_weight, up_weight, down_weight, saved_gate, saved_up,
):
    NG, NI, NZ = lax.axis_size("group"), lax.axis_size("inner"), lax.axis_size("dp")
    NB = NG * NI
    tokens, D = token_inputs.shape
    E = router_weight.shape[1]
    K = expert_ids.shape[1]
    F = down_weight.shape[1]
    S = saved_gate.shape[1]
    T = NB * tokens
    FS = D // NZ
    FP = -(-(FS + K) // 128) * 128
    half = NZ // 2
    n = lax.axis_index("dp")

    matches = (expert_ids[:, :, None] == jnp.arange(E, dtype=jnp.int32)).astype(jnp.int32)
    per_token = jnp.sum(matches, axis=1)
    earlier = jnp.cumsum(per_token, axis=0) - per_token
    position = jnp.sum(matches * earlier[:, None, :], axis=2)
    codes = (expert_ids + E * position).astype(bf16)
    code_rows = (per_token * (1 + earlier)).astype(bf16)
    grad_cols = lax.dynamic_slice_in_dim(out_grads, n * FS, FS, 1)
    tok_cols = lax.dynamic_slice_in_dim(token_inputs, n * FS, FS, 1)
    pay1 = jnp.concatenate((grad_cols, codes, jnp.zeros((tokens, FP - FS - K), bf16)), axis=1)
    pay2 = jnp.concatenate((tok_cols, jnp.zeros((tokens, FP - FS), bf16), code_rows), axis=1)
    scores = jnp.dot(token_inputs.astype(f32), router_weight, precision=HI)

    vmem = pl.BlockSpec(memory_space=pltpu.VMEM)
    hbm = pl.BlockSpec(memory_space=pl.ANY)
    V = pltpu.VMEM
    dma = pltpu.SemaphoreType.DMA
    scratch = [
        V((2, F, D), bf16), V((2, F, D), bf16), V((2, F, D), bf16),
        V((2, F, S), bf16), V((2, F, S), bf16), V((FS, E), f32),
        V((NG, NI, 16, FP), bf16), V((NG, NI, 16, FP + E), bf16), V((NG, NI, 16, E), f32),
        V((2 * S, T), bf16), V((NG, NI, 16, 2 * S), bf16), V((2, D, 2 * F), bf16),
        V((FS, T), bf16), V((NZ, FS, 2 * S), bf16), V((2, 2, F, S), f32),
        V((NZ, 2, S), f32), V((NG, NI, 2, S), f32), V((E, S), f32), V((S, E), f32),
        V((NB, 16, E), f32),
        V((2, half, FS, 2 * S), bf16), V((2, half, FS, 2 * S), bf16), V((FP, 2 * S), bf16),
        V((NI, NG, 16, FP), bf16), V((NI, NG, 16, FP), bf16), V((NG, 16, FP), bf16),
        V((NG, 16, FP), f32), V((NG, 16, FP), bf16),
        dma((6,)), dma((5, NG)), dma((5, NG)), dma((5, NI)), dma((5, NI)),
        dma((2, half, CHUNKS)), dma((2, half, CHUNKS)),
        dma((2, half, CHUNKS)), dma((2, half, CHUNKS)),
        dma((NZ,)), dma((NZ,)),
    ]
    return pl.pallas_call(
        functools.partial(kernel, NZ, NG, NI, K),
        out_shape=(
            jax.ShapeDtypeStruct((tokens, FS), bf16),
            jax.ShapeDtypeStruct((FS, E), f32),
        ),
        in_specs=[vmem] * 3 + [hbm] * 6,
        out_specs=(vmem, vmem),
        scratch_shapes=scratch,
        compiler_params=pltpu.CompilerParams(
            collective_id=0, has_side_effects=True, vmem_limit_bytes=40 * 1024 * 1024
        ),
        name="expert_backward",
    )(
        pay1, pay2, scores, router_weight,
        jnp.swapaxes(gate_weight, 1, 2), jnp.swapaxes(up_weight, 1, 2), down_weight,
        jnp.swapaxes(saved_gate, 1, 2), jnp.swapaxes(saved_up, 1, 2),
    )


def solution(mesh):
    placed = (
        P(("group", "inner"), None),
        P(("group", "inner"), None),
        P(("group", "inner"), None),
        P(),
        P(("group", "inner"), None, "dp"),
        P(("group", "inner"), None, "dp"),
        P(("group", "inner"), "dp", None),
        P(("group", "inner"), None, "dp"),
        P(("group", "inner"), None, "dp"),
    )
    return jax.shard_map(
        local,
        mesh=mesh,
        in_specs=placed,
        out_specs=(P(("group", "inner"), "dp"), P("dp", None)),
        check_vma=False,
    )
```

```python
import functools

import jax
import jax.numpy as jnp
from jax import lax
from jax.experimental import pallas as pl
from jax.experimental.pallas import tpu as pltpu
from jax.sharding import PartitionSpec as P

MESH = pl.DeviceIdType.MESH
route_scale = 2.5
f32, bf16 = jnp.float32, jnp.bfloat16
HI = lax.Precision.HIGHEST


def dot_nt(a, b, **kw):
    return lax.dot_general(a, b, (((1,), (1,)), ((), ())), preferred_element_type=f32, **kw)


def dot_nn(a, b):
    return lax.dot_general(a, b, (((1,), (0,)), ((), ())), preferred_element_type=f32)


def iota(shape, dim):
    return lax.broadcasted_iota(jnp.int32, shape, dim)


def kernel(
    NZ, NG, NI, K,
    pay1, pay2, tok, rw_hbm, gw_hbm, uw_hbm, dw_hbm, sg_hbm, su_hbm,
    out_x, out_r,
    gwv, uwv, dwv, sgv, suv, rwv, dws,
    buf1, buf2, buf3, pt, pmix, wT, tokT, xt, dgu, gz, bufG, gflat, gt, lg,
    rs_src, rs_dst, finv, tbuf, rbuf, ysrc, yacc, ydst,
    load_sem, ys, yr, xs, xr, ag_s, ag_r, rs_s, rs_r, z_s, z_r,
):
    NB = NG * NI
    T = 16 * NB
    S = 2 * NB
    E = 2 * NB
    FP = pay1.shape[1]
    F = dwv.shape[1]
    D = dwv.shape[2]
    FS = D // NZ
    half = NZ // 2
    CR = FS // 2
    g, i, n = lax.axis_index("group"), lax.axis_index("inner"), lax.axis_index("dp")
    q = g * NI + i

    load_rw = pltpu.make_async_copy(rw_hbm, rwv, load_sem.at[0])
    loads = [
        pltpu.make_async_copy(dw_hbm, dwv, load_sem.at[1]),
        pltpu.make_async_copy(sg_hbm, sgv, load_sem.at[2]),
        pltpu.make_async_copy(su_hbm, suv, load_sem.at[3]),
    ]
    loads_w = [
        pltpu.make_async_copy(gw_hbm, gwv, load_sem.at[4]),
        pltpu.make_async_copy(uw_hbm, uwv, load_sem.at[5]),
    ]

    def each(count, fn):
        def body(r, carry):
            fn(r)
            return carry

        lax.fori_loop(1, count, body, 0)

    def peer(axis, r):
        me, size = {"group": (g, NG), "inner": (i, NI), "dp": (n, NZ)}[axis]
        return {axis: lax.rem(me + r, size)}

    bar = pltpu.get_barrier_semaphore()
    for axis, offsets in (("dp", (1, NZ - 1)), ("group", range(1, NG)), ("inner", range(1, NI))):
        for r in offsets:
            pl.semaphore_signal(bar, inc=1, device_id=peer(axis, r), device_id_type=MESH)
    load_rw.start()
    for c in loads + loads_w:
        c.start()
    pl.semaphore_wait(bar, NG + NI)

    def remote(src, dst, s, r, dev):
        return pltpu.make_async_remote_copy(
            src_ref=src, dst_ref=dst, send_sem=s, recv_sem=r, device_id=dev, device_id_type=MESH
        )

    def y_copy(t, r):
        src, dst = ((pay1, buf1), (pay2, buf2), (None, buf3))[t]
        src = buf3.at[g, i] if src is None else src
        return remote(src, dst.at[g, i], ys.at[t], yr.at[t], peer("group", r))

    def y_all(t):
        ref = (buf1, buf2, buf3)[t].at[pl.ds(0, NG - 1), i]
        return remote(ref, ref, ys.at[t], yr.at[t], peer("group", 1))

    def x_copy(t, r):
        buf = (buf1, buf2, buf3)[t]
        return remote(buf.at[:, i], buf.at[:, i], xs.at[t], xr.at[t], peer("inner", r))

    def x_all(t):
        ref = (buf1, buf2, buf3)[t].at[:, pl.ds(0, NI - 1)]
        return remote(ref, ref, xs.at[t], xr.at[t], peer("inner", 1))

    each(NG, lambda r: y_copy(0, r).start())
    buf1[g, i] = pay1[...]
    each(NG, lambda r: y_copy(1, r).start())
    buf2[g, i] = pay2[...]
    load_rw.wait()
    parts = 7 if D % (7 * 128) == 0 else half
    cols = D // parts
    scores = None
    for p in range(parts):
        rest = rwv[p * cols : (p + 1) * cols, :]
        left = tok[:, p * cols : (p + 1) * cols]
        for _ in range(3):
            top = rest.astype(bf16)
            term = dot_nn(left, top)
            scores = term if scores is None else scores + term
            rest = rest - top.astype(f32)
    buf3[g, i] = scores
    each(NG, lambda r: y_copy(2, r).start())
    for c in loads:
        c.wait()
    for j in range(2):
        a = sgv[j].astype(f32)
        u = suv[j].astype(f32)
        sig = jax.nn.sigmoid(a)
        dgu[j, 0] = u * sig * (1.0 + a * (1.0 - sig))
        dgu[j, 1] = a * sig

    y_all(0).wait_recv()
    each(NI, lambda r: x_copy(0, r).start())
    down = dwv[...].reshape(2 * F, D)
    for m in range(NZ):
        dws[m, :, 0:FS] = down[:, m * FS : (m + 1) * FS]
    for c in loads_w:
        c.wait()
    for p in range(parts):
        cut = slice(p * cols, (p + 1) * cols)
        rows = jnp.concatenate((gwv[0, :, cut], uwv[0, :, cut], gwv[1, :, cut], uwv[1, :, cut]), axis=0)
        wT[cut, :] = rows.astype(f32).T.astype(bf16)
    x_all(0).wait_recv()

    X = buf1[...].reshape(T, FP)
    sel = (iota((16, FP), 1) == iota((16, FP), 0) + FS).astype(bf16)
    codes = dot_nt(sel, X)
    srow = iota((S, T), 0)
    same = (srow >> 1) == (iota((S, T), 1) >> 4)
    for j in range(2):
        want = (2 * q + j + E * (iota((S, 1), 0) & 1)).astype(f32)
        hit = codes[0:1] == want
        for k in range(1, K):
            hit = hit | (codes[k : k + 1] == want)
        pt[pl.ds(j * S, S), :] = jnp.where(same & hit, 1.0, 0.0).astype(bf16)
    xs_rows = dot_nn(pt[...], X)
    xt[n] = xs_rows.T[0:FS].astype(bf16)

    def rows_of(c):
        return pl.ds((c // 2) * CR, CR)

    def lanes_of(c):
        return pl.ds((c % 2) * S, S)

    def zdev(d):
        return {"dp": lax.rem(n + (1 if d == 0 else NZ - 1), NZ)}

    def behind(d, st):
        return lax.rem(n + (NZ - st if d == 0 else st), NZ)

    def ag_copy(d, st, c):
        ref = xt.at[behind(d, st), rows_of(c), lanes_of(c)]
        return remote(ref, ref, ag_s.at[d, c], ag_r.at[d, st, c], zdev(d))

    def ag_sent(d, c):
        ref = xt.at[pl.ds(0, half if c // 2 == d else half - 1), rows_of(c), lanes_of(c)]
        return remote(ref, ref, ag_s.at[d, c], ag_r.at[d, 0, c], zdev(d))

    def ag_has(d, st, c):
        return st < half - 1 or c // 2 == d

    def mix_tokens():
        codes_all = buf2[:, :, :, FP : FP + E].reshape(T, E).astype(f32)
        aff = jax.nn.sigmoid(buf3[...].reshape(T, E))
        named = jnp.where(codes_all > 0.0, aff, 0.0)
        mix = (route_scale * named / jnp.sum(named, axis=1, keepdims=True)).astype(bf16)
        owner = (iota((E, 2 * S), 1) >= S).astype(jnp.int32) + 2 * q
        pick = (iota((E, 2 * S), 0) == owner).astype(bf16)
        spread = dot_nn(mix, pick)
        placed = pt[...].astype(f32).T
        pmix[...] = (placed * spread).astype(bf16).reshape(NG, NI, 16, 2 * S)

    def token_transpose():
        rows = buf2[:, :, :, 0:FP].reshape(T, FP)
        tokT[...] = rows.astype(f32).T[0:FS].astype(bf16)

    def hidden_term(m):
        return dot_nn(dws[m, :, 0:FS], xt[m])

    hid = None
    for st in range(half):
        for c in range(4):
            for d in range(2):
                if st > 0:
                    ag_copy(d, st - 1, c).wait_recv()
                if ag_has(d, st, c):
                    ag_copy(d, st, c).start()
        if st == 0:
            y_all(1).wait_recv()
            y_all(2).wait_recv()
            each(NI, lambda r: x_copy(1, r).start())
            each(NI, lambda r: x_copy(2, r).start())
            hid = hidden_term(n)
        else:
            hid = hid + hidden_term(behind(0, st)) + hidden_term(behind(1, st))
        if st == min(3, half - 1):
            x_all(1).wait_recv()
            x_all(2).wait_recv()
            mix_tokens()
        if st == min(4, half - 1):
            token_transpose()
    for d in range(2):
        for c in range(4):
            if ag_has(d, half - 1, c):
                ag_copy(d, half - 1, c).wait_recv()
    hid = hid + hidden_term(behind(0, half))

    both = []
    for j in range(2):
        h = hid[j * F : (j + 1) * F, j * S : (j + 1) * S]
        up = h * dgu[j, 1]
        gz[n, pl.ds(j, 1), :] = jnp.sum(up * suv[j].astype(f32), axis=0, keepdims=True)
        pair = jnp.concatenate((h * dgu[j, 0], up), axis=0).astype(bf16)
        none = jnp.zeros_like(pair)
        both.append(jnp.concatenate((pair, none) if j == 0 else (none, pair), axis=1))
    grads_t = jnp.concatenate(both, axis=0)

    def part(m):
        return dot_nn(wT[pl.ds(pl.multiple_of(m * FS, 16), FS), :], grads_t)

    def z_copy(d, st):
        ref = gz.at[behind(d, st)]
        return remote(ref, ref, z_s.at[d], z_r.at[d, st], zdev(d))

    def z_sent(d):
        ref = gz.at[pl.ds(0, half - d)]
        return remote(ref, ref, z_s.at[d], z_r.at[d, 0], zdev(d))

    def gx_copy(r):
        return remote(bufG.at[g, i], bufG.at[g, i], xs.at[3], xr.at[3], peer("inner", r))

    def gx_all():
        ref = bufG.at[g, pl.ds(0, NI - 1)]
        return remote(ref, ref, xs.at[3], xr.at[3], peer("inner", 1))

    def gy_copy(r):
        return remote(bufG.at[g], bufG.at[g], ys.at[3], yr.at[3], peer("group", r))

    def gy_all():
        ref = bufG.at[pl.ds(0, NG - 1)]
        return remote(ref, ref, ys.at[3], yr.at[3], peer("group", 1))

    def router_side():
        for b in range(NB):
            gflat[2 * b : 2 * b + 2, :] = bufG[b // NI, b % NI]
        gt[...] = gflat[...].T

        def body(b, carry):
            gb, ib = b // NI, lax.rem(b, NI)
            code = buf2[gb, ib, :, FP : FP + E].astype(f32)
            aff = jax.nn.sigmoid(buf3[gb, ib])
            g0 = gt[pl.ds(2 * b, 1), :]
            g1 = gt[pl.ds(2 * b + 1, 1), :]
            grads = jnp.where(code == 1.0, g0, jnp.where(code == 2.0, g1, 0.0))
            named = jnp.where(code > 0.0, aff, 0.0)
            total = jnp.sum(named, axis=1, keepdims=True)
            weighted = jnp.sum(named * grads, axis=1, keepdims=True)
            lg[b] = route_scale * (grads / total - weighted / (total * total)) * named * (1.0 - aff)
            return carry

        lax.fori_loop(0, NB, body, 0, unroll=8)

    def router_product():
        rest = lg[...].reshape(T, E)
        acc = None
        for _ in range(3):
            top = rest.astype(bf16)
            term = dot_nn(tokT[...], top)
            acc = term if acc is None else acc + term
            rest = rest - top.astype(f32)
        out_r[...] = acc

    def rs_copy(d, st, c):
        return remote(
            rs_src.at[d, st, rows_of(c), lanes_of(c)], rs_dst.at[d, st, rows_of(c), lanes_of(c)],
            rs_s.at[d, c], rs_r.at[d, st, c], zdev(d),
        )

    def rs_sent(d, c):
        cut = (d, pl.ds(0, half if c // 2 == d else half - 1), rows_of(c), lanes_of(c))
        return remote(rs_src.at[cut], rs_dst.at[cut], rs_s.at[d, c], rs_r.at[d, 0, c], zdev(d))

    def rs_has(d, st, c):
        return st > 0 or c // 2 == d

    def cut_of(value, c):
        return value[(c // 2) * CR : (c // 2 + 1) * CR, (c % 2) * S : (c % 2 + 1) * S]

    for st in range(half):
        ahead = [part(behind(1 - d, half - st)) for d in range(2)] if st else [part(behind(0, half))] * 2
        for d in range(2):
            if st > 0:
                z_copy(d, st - 1).wait_recv()
            if st < half - d:
                z_copy(d, st).start()
        for cc in range(4):
            for d in range(2):
                c = cc if d == 0 else (cc + 2) % 4
                if not rs_has(d, st, c):
                    continue
                acc = cut_of(ahead[d], c)
                if st > 0 and rs_has(d, st - 1, c):
                    rs_copy(d, st - 1, c).wait_recv()
                    acc = acc + rs_dst[d, st - 1, rows_of(c), lanes_of(c)].astype(f32)
                rs_src[d, st, rows_of(c), lanes_of(c)] = acc.astype(bf16)
                rs_copy(d, st, c).start()

    mine = part(n)
    z_copy(0, half - 1).wait_recv()
    bufG[g, i] = jnp.sum(gz[...], axis=0)
    each(NI, lambda r: gx_copy(r).start())
    for c in range(4):
        acc = cut_of(mine, c)
        for d in range(2):
            if rs_has(d, half - 1, c):
                rs_copy(d, half - 1, c).wait_recv()
                acc = acc + rs_dst[d, half - 1, rows_of(c), lanes_of(c)].astype(f32)
        finv[rows_of(c), lanes_of(c)] = acc.astype(bf16)
    if FP > FS:
        finv[FS:FP, :] = jnp.zeros((FP - FS, 2 * S), bf16)

    def tx_copy(r):
        return remote(tbuf.at[r], rbuf.at[r], xs.at[4], xr.at[4], peer("inner", r))

    def tx_all():
        cut = pl.ds(1, NI - 1)
        return remote(tbuf.at[cut], rbuf.at[cut], xs.at[4], xr.at[4], peer("inner", 1))

    def ty_copy(r):
        to = lax.rem(g + r, NG)
        return remote(ysrc.at[to], ydst.at[r], ys.at[4], yr.at[4], peer("group", r))

    def ty_all():
        return remote(
            ysrc.at[pl.ds(0, NG - 1)], ydst.at[pl.ds(1, NG - 1)], ys.at[4], yr.at[4], peer("group", 1)
        )

    def token_rows(at):
        return dot_nt(pmix[:, at].reshape(NG * 16, 2 * S), finv[...])

    def send_rows(r):
        tbuf[r] = token_rows(lax.rem(i + r, NI)).astype(bf16).reshape(NG, 16, FP)
        tx_copy(r).start()

    each(NI, send_rows)
    acc = token_rows(i)
    gx_all().wait_recv()
    each(NG, lambda r: gy_copy(r).start())
    tx_all().wait_recv()
    for r in range(1, NI):
        acc = acc + rbuf[r].astype(f32).reshape(NG * 16, FP)
    yacc[...] = acc.reshape(NG, 16, FP)
    ysrc[...] = acc.astype(bf16).reshape(NG, 16, FP)
    each(NG, lambda r: ty_copy(r).start())
    gy_all().wait_recv()
    router_side()
    extra = dot_nt(lg[q], rwv[pl.ds(pl.multiple_of(n * FS, 8), FS), :], precision=HI)
    router_product()
    total = yacc[g]
    ty_all().wait_recv()
    for r in range(1, NG):
        total = total + ydst[r].astype(f32)
    out_x[...] = (total[:, 0:FS] + extra).astype(bf16)

    for t in range(3):
        y_all(t).wait_send()
        x_all(t).wait_send()
    gx_all().wait_send()
    gy_all().wait_send()
    tx_all().wait_send()
    ty_all().wait_send()
    for d in range(2):
        z_sent(d).wait_send()
        for c in range(4):
            ag_sent(d, c).wait_send()
            rs_sent(d, c).wait_send()


def local(
    token_inputs, out_grads, expert_ids, router_weight,
    gate_weight, up_weight, down_weight, saved_gate, saved_up,
):
    NG, NI, NZ = lax.axis_size("group"), lax.axis_size("inner"), lax.axis_size("dp")
    NB = NG * NI
    tokens, D = token_inputs.shape
    E = router_weight.shape[1]
    K = expert_ids.shape[1]
    F = down_weight.shape[1]
    S = saved_gate.shape[1]
    T = NB * tokens
    FS = D // NZ
    FP = -(-(FS + K) // 128) * 128
    half = NZ // 2
    n = lax.axis_index("dp")

    matches = (expert_ids[:, :, None] == jnp.arange(E, dtype=jnp.int32)).astype(jnp.int32)
    per_token = jnp.sum(matches, axis=1)
    earlier = jnp.cumsum(per_token, axis=0) - per_token
    position = jnp.sum(matches * earlier[:, None, :], axis=2)
    codes = (expert_ids + E * position).astype(bf16)
    code_rows = (per_token * (1 + earlier)).astype(bf16)
    grad_cols = lax.dynamic_slice_in_dim(out_grads, n * FS, FS, 1)
    tok_cols = lax.dynamic_slice_in_dim(token_inputs, n * FS, FS, 1)
    pay1 = jnp.concatenate((grad_cols, codes, jnp.zeros((tokens, FP - FS - K), bf16)), axis=1)
    pay2 = jnp.concatenate((tok_cols, jnp.zeros((tokens, FP - FS), bf16), code_rows), axis=1)

    vmem = pl.BlockSpec(memory_space=pltpu.VMEM)
    hbm = pl.BlockSpec(memory_space=pl.ANY)
    V = pltpu.VMEM
    dma = pltpu.SemaphoreType.DMA
    scratch = [
        V((2, F, D), bf16), V((2, F, D), bf16), V((2, F, D), bf16),
        V((2, F, S), bf16), V((2, F, S), bf16), V((D, E), f32), V((NZ, 2 * F, FP), bf16),
        V((NG, NI, 16, FP), bf16), V((NG, NI, 16, FP + E), bf16), V((NG, NI, 16, E), f32),
        V((2 * S, T), bf16), V((NG, NI, 16, 2 * S), bf16), V((D, 4 * F), bf16),
        V((FS, T), bf16), V((NZ, FS, 2 * S), bf16), V((2, 2, F, S), f32),
        V((NZ, 2, S), f32), V((NG, NI, 2, S), f32), V((E, S), f32), V((S, E), f32),
        V((NB, 16, E), f32),
        V((2, half, FS, 2 * S), bf16), V((2, half, FS, 2 * S), bf16), V((FP, 2 * S), bf16),
        V((NI, NG, 16, FP), bf16), V((NI, NG, 16, FP), bf16), V((NG, 16, FP), bf16),
        V((NG, 16, FP), f32), V((NG, 16, FP), bf16),
        dma((6,)), dma((5,)), dma((5,)), dma((5,)), dma((5,)),
        dma((2, 4)), dma((2, half, 4)), dma((2, 4)), dma((2, half, 4)),
        dma((2,)), dma((2, half)),
    ]
    return pl.pallas_call(
        functools.partial(kernel, NZ, NG, NI, K),
        out_shape=(
            jax.ShapeDtypeStruct((tokens, FS), bf16),
            jax.ShapeDtypeStruct((FS, E), f32),
        ),
        in_specs=[vmem] * 3 + [hbm] * 6,
        out_specs=(vmem, vmem),
        scratch_shapes=scratch,
        compiler_params=pltpu.CompilerParams(
            collective_id=0, has_side_effects=True, vmem_limit_bytes=58 * 1024 * 1024
        ),
        name="expert_backward",
    )(
        pay1, pay2, token_inputs, router_weight,
        jnp.swapaxes(gate_weight, 1, 2), jnp.swapaxes(up_weight, 1, 2), down_weight,
        jnp.swapaxes(saved_gate, 1, 2), jnp.swapaxes(saved_up, 1, 2),
    )


def solution(mesh):
    placed = (
        P(("group", "inner"), None),
        P(("group", "inner"), None),
        P(("group", "inner"), None),
        P(),
        P(("group", "inner"), None, "dp"),
        P(("group", "inner"), None, "dp"),
        P(("group", "inner"), "dp", None),
        P(("group", "inner"), None, "dp"),
        P(("group", "inner"), None, "dp"),
    )
    return jax.shard_map(
        local,
        mesh=mesh,
        in_specs=placed,
        out_specs=(P(("group", "inner"), "dp"), P("dp", None)),
        check_vma=False,
    )
```

```python
import functools

import jax
import jax.numpy as jnp
from jax import lax
from jax.experimental import pallas as pl
from jax.experimental.pallas import tpu as pltpu
from jax.sharding import PartitionSpec as P

MESH = pl.DeviceIdType.MESH
route_scale = 2.5
f32, bf16 = jnp.float32, jnp.bfloat16
HI = lax.Precision.HIGHEST


def dot_nt(a, b, **kw):
    return lax.dot_general(a, b, (((1,), (1,)), ((), ())), preferred_element_type=f32, **kw)


def dot_nn(a, b):
    return lax.dot_general(a, b, (((1,), (0,)), ((), ())), preferred_element_type=f32)


def iota(shape, dim):
    return lax.broadcasted_iota(jnp.int32, shape, dim)


def kernel(
    NZ, NG, NI, K,
    ids, grads, tok, rw_hbm, gw_hbm, uw_hbm, dw_hbm, sg_hbm, su_hbm,
    out_x, out_r,
    gwv, uwv, dwv, sgv, suv, rwv, dws,
    buf1, buf2, buf3, pt, pmix, wT, tokT, xt, dgu, gz, bufG, gflat, gt, lg,
    rs_src, rs_dst, finv, tbuf, rbuf, ysrc, yacc, ydst,
    load_sem, ys, yr, xs, xr, ag_s, ag_r, rs_s, rs_r, z_s, z_r,
):
    NB = NG * NI
    T = 16 * NB
    S = 2 * NB
    E = 2 * NB
    FP = buf1.shape[3]
    F = dwv.shape[1]
    D = dwv.shape[2]
    FS = D // NZ
    half = NZ // 2
    CR = FS // 2
    JUMP = 3 if half >= 5 else 0
    g, i, n = lax.axis_index("group"), lax.axis_index("inner"), lax.axis_index("dp")
    q = g * NI + i

    load_rw = pltpu.make_async_copy(rw_hbm, rwv, load_sem.at[0])
    loads = [
        pltpu.make_async_copy(dw_hbm, dwv, load_sem.at[1]),
        pltpu.make_async_copy(sg_hbm, sgv, load_sem.at[2]),
        pltpu.make_async_copy(su_hbm, suv, load_sem.at[3]),
    ]
    loads_w = [
        pltpu.make_async_copy(gw_hbm, gwv, load_sem.at[4]),
        pltpu.make_async_copy(uw_hbm, uwv, load_sem.at[5]),
    ]

    def each(count, fn):
        def body(r, carry):
            fn(r)
            return carry

        lax.fori_loop(1, count, body, 0)

    def peer(axis, r):
        me, size = {"group": (g, NG), "inner": (i, NI), "dp": (n, NZ)}[axis]
        return {axis: lax.rem(me + r, size)}

    bar = pltpu.get_barrier_semaphore()
    zpeers = (1, NZ - 1) + ((JUMP, NZ - JUMP) if JUMP else ())
    for axis, offsets in (("dp", zpeers), ("group", range(1, NG)), ("inner", range(1, NI))):
        for r in offsets:
            pl.semaphore_signal(bar, inc=1, device_id=peer(axis, r), device_id_type=MESH)
    load_rw.start()
    for c in loads + loads_w:
        c.start()

    lane_e = iota((16, E), 1).astype(f32)
    eye = (iota((16, 16), 1) == iota((16, 16), 0)).astype(bf16)
    named_ids = dot_nt(eye, ids[...].astype(f32).astype(bf16))
    hits = [named_ids[:, k : k + 1] == lane_e for k in range(K)]
    per_token = jnp.where(hits[0], 1.0, 0.0)
    for k in range(1, K):
        per_token = per_token + jnp.where(hits[k], 1.0, 0.0)
    lower = (iota((16, 16), 1) < iota((16, 16), 0)).astype(bf16)
    earlier = dot_nn(lower, per_token.astype(bf16))
    lane_p = iota((16, FP), 1)
    turn = lax.rem(D - n * FS, D)

    def columns(ref):
        return jnp.where(lane_p < FS, pltpu.roll(ref[...].astype(f32), turn, 1)[:, 0:FP], 0.0)

    rows1 = columns(grads)
    for k in range(K):
        position = jnp.sum(jnp.where(hits[k], earlier, 0.0), axis=1, keepdims=True)
        code = named_ids[:, k : k + 1] + E * position
        rows1 = jnp.where(lane_p == FS + k, code, rows1)
    buf1[g, i] = rows1.astype(bf16)
    buf2[g, i, :, 0:FP] = columns(tok).astype(bf16)
    buf2[g, i, :, FP : FP + E] = (per_token * (1.0 + earlier)).astype(bf16)
    pl.semaphore_wait(bar, NG + NI - 2 + len(zpeers))

    def remote(src, dst, s, r, dev):
        return pltpu.make_async_remote_copy(
            src_ref=src, dst_ref=dst, send_sem=s, recv_sem=r, device_id=dev, device_id_type=MESH
        )

    def y_copy(t, r):
        ref = (buf1, buf2, buf3)[t].at[g, i]
        return remote(ref, ref, ys.at[t], yr.at[t], peer("group", r))

    def y_all(t):
        ref = (buf1, buf2, buf3)[t].at[pl.ds(0, NG - 1), i]
        return remote(ref, ref, ys.at[t], yr.at[t], peer("group", 1))

    def x_copy(t, r):
        buf = (buf1, buf2, buf3)[t]
        return remote(buf.at[:, i], buf.at[:, i], xs.at[t], xr.at[t], peer("inner", r))

    def x_all(t):
        ref = (buf1, buf2, buf3)[t].at[:, pl.ds(0, NI - 1)]
        return remote(ref, ref, xs.at[t], xr.at[t], peer("inner", 1))

    each(NG, lambda r: y_copy(0, r).start())
    each(NG, lambda r: y_copy(1, r).start())
    load_rw.wait()
    parts = 7 if D % (7 * 128) == 0 else half
    cols = D // parts
    scores = None
    for p in range(parts):
        rest = rwv[p * cols : (p + 1) * cols, :]
        left = tok[:, p * cols : (p + 1) * cols]
        for _ in range(3):
            top = rest.astype(bf16)
            term = dot_nn(left, top)
            scores = term if scores is None else scores + term
            rest = rest - top.astype(f32)
    buf3[g, i] = scores
    each(NG, lambda r: y_copy(2, r).start())
    for c in loads:
        c.wait()
    for j in range(2):
        a = sgv[j].astype(f32)
        u = suv[j].astype(f32)
        sig = jax.nn.sigmoid(a)
        dgu[j, 0] = u * sig * (1.0 + a * (1.0 - sig))
        dgu[j, 1] = a * sig

    y_all(0).wait_recv()
    each(NI, lambda r: x_copy(0, r).start())
    down = dwv[...].reshape(2 * F, D)
    for m in range(NZ):
        dws[m, :, 0:FS] = down[:, m * FS : (m + 1) * FS]
    for c in loads_w:
        c.wait()
    for p in range(parts):
        cut = slice(p * cols, (p + 1) * cols)
        rows = jnp.concatenate((gwv[0, :, cut], uwv[0, :, cut], gwv[1, :, cut], uwv[1, :, cut]), axis=0)
        wT[cut, :] = rows.astype(f32).T.astype(bf16)
    x_all(0).wait_recv()

    X = buf1[...].reshape(T, FP)
    sel = (iota((16, FP), 1) == iota((16, FP), 0) + FS).astype(bf16)
    codes = dot_nt(sel, X)
    srow = iota((S, T), 0)
    same = (srow >> 1) == (iota((S, T), 1) >> 4)
    for j in range(2):
        want = (2 * q + j + E * (iota((S, 1), 0) & 1)).astype(f32)
        hit = codes[0:1] == want
        for k in range(1, K):
            hit = hit | (codes[k : k + 1] == want)
        pt[pl.ds(j * S, S), :] = jnp.where(same & hit, 1.0, 0.0).astype(bf16)
    xs_rows = dot_nn(pt[...], X)
    xt[n] = xs_rows.T[0:FS].astype(bf16)

    def rows_of(c):
        return pl.ds((c // 2) * CR, CR)

    def lanes_of(c):
        return pl.ds((c % 2) * S, S)

    def zdev(d, dist):
        by = dist if dist == JUMP else 1
        return {"dp": lax.rem(n + (by if d == 0 else NZ - by), NZ)}

    def behind(d, st):
        return lax.rem(n + (NZ - st if d == 0 else st), NZ)

    def held(d, dist):
        return n if dist == JUMP else behind(d, dist - 1)

    if JUMP:
        chains = [list(range(JUMP, half + 1)), list(range(1, JUMP))]
    else:
        chains = [list(range(1, half + 1))]
    plan = [[(None, ch[0]) for ch in chains]]
    for st in range(1, len(chains[0]) + 1):
        plan.append(
            [(ch[st - 1], ch[st] if st < len(ch) else None) for ch in chains if st <= len(ch)]
        )

    def ag_copy(d, dist, c):
        ref = xt.at[held(d, dist), rows_of(c), lanes_of(c)]
        return remote(ref, ref, ag_s.at[d, c], ag_r.at[d, dist - 1, c], zdev(d, dist))

    def ag_sent(d, c):
        ref = xt.at[pl.ds(0, half if c // 2 == d else half - 1), rows_of(c), lanes_of(c)]
        return remote(ref, ref, ag_s.at[d, c], ag_r.at[d, 0, c], zdev(d, 1))

    def ag_has(d, dist, c):
        return dist < half or c // 2 == d

    def mix_tokens():
        codes_all = buf2[:, :, :, FP : FP + E].reshape(T, E).astype(f32)
        aff = jax.nn.sigmoid(buf3[...].reshape(T, E))
        named = jnp.where(codes_all > 0.0, aff, 0.0)
        mix = (route_scale * named / jnp.sum(named, axis=1, keepdims=True)).astype(bf16)
        owner = (iota((E, 2 * S), 1) >= S).astype(jnp.int32) + 2 * q
        pick = (iota((E, 2 * S), 0) == owner).astype(bf16)
        spread = dot_nn(mix, pick)
        placed = pt[...].astype(f32).T
        pmix[...] = (placed * spread).astype(bf16).reshape(NG, NI, 16, 2 * S)

    def token_transpose():
        rows = buf2[:, :, :, 0:FP].reshape(T, FP)
        tokT[...] = rows.astype(f32).T[0:FS].astype(bf16)

    def hidden_term(m):
        return dot_nn(dws[m, :, 0:FS], xt[m])

    hid = None
    for st, moves in enumerate(plan):
        for came, goes in moves:
            for c in range(4):
                for d in range(2):
                    if came is not None and ag_has(d, came, c):
                        ag_copy(d, came, c).wait_recv()
                    if goes is not None and ag_has(d, goes, c):
                        ag_copy(d, goes, c).start()
        if st == 0:
            y_all(1).wait_recv()
            y_all(2).wait_recv()
            each(NI, lambda r: x_copy(1, r).start())
            each(NI, lambda r: x_copy(2, r).start())
            hid = hidden_term(n)
        for came, goes in moves:
            if came is not None:
                hid = hid + hidden_term(behind(0, came))
                if came < half:
                    hid = hid + hidden_term(behind(1, came))
        if st == len(plan) - 2:
            x_all(1).wait_recv()
            token_transpose()

    both = []
    for j in range(2):
        h = hid[j * F : (j + 1) * F, j * S : (j + 1) * S]
        up = h * dgu[j, 1]
        gz[n, pl.ds(j, 1), :] = jnp.sum(up * suv[j].astype(f32), axis=0, keepdims=True)
        pair = jnp.concatenate((h * dgu[j, 0], up), axis=0).astype(bf16)
        none = jnp.zeros_like(pair)
        both.append(jnp.concatenate((pair, none) if j == 0 else (none, pair), axis=1))
    grads_t = jnp.concatenate(both, axis=0)

    def part(m):
        return dot_nn(wT[pl.ds(pl.multiple_of(m * FS, 16), FS), :], grads_t)

    def z_copy(d, dist):
        ref = gz.at[held(d, dist)]
        return remote(ref, ref, z_s.at[d], z_r.at[d, dist - 1], zdev(d, dist))

    def z_sent(d):
        ref = gz.at[pl.ds(0, half - d)]
        return remote(ref, ref, z_s.at[d], z_r.at[d, 0], zdev(d, 1))

    def z_step(st):
        for came, goes in plan[st]:
            for d in range(2):
                if came is not None and came <= half - d:
                    z_copy(d, came).wait_recv()
                if goes is not None and goes <= half - d:
                    z_copy(d, goes).start()

    def gx_copy(r):
        return remote(bufG.at[g, i], bufG.at[g, i], xs.at[3], xr.at[3], peer("inner", r))

    def gx_all():
        ref = bufG.at[g, pl.ds(0, NI - 1)]
        return remote(ref, ref, xs.at[3], xr.at[3], peer("inner", 1))

    def gy_copy(r):
        return remote(bufG.at[g], bufG.at[g], ys.at[3], yr.at[3], peer("group", r))

    def gy_all():
        ref = bufG.at[pl.ds(0, NG - 1)]
        return remote(ref, ref, ys.at[3], yr.at[3], peer("group", 1))

    def router_side():
        for b in range(NB):
            gflat[2 * b : 2 * b + 2, :] = bufG[b // NI, b % NI]
        gt[...] = gflat[...].T

        def body(b, carry):
            gb, ib = b // NI, lax.rem(b, NI)
            code = buf2[gb, ib, :, FP : FP + E].astype(f32)
            aff = jax.nn.sigmoid(buf3[gb, ib])
            g0 = gt[pl.ds(2 * b, 1), :]
            g1 = gt[pl.ds(2 * b + 1, 1), :]
            grads = jnp.where(code == 1.0, g0, jnp.where(code == 2.0, g1, 0.0))
            named = jnp.where(code > 0.0, aff, 0.0)
            total = jnp.sum(named, axis=1, keepdims=True)
            weighted = jnp.sum(named * grads, axis=1, keepdims=True)
            lg[b] = route_scale * (grads / total - weighted / (total * total)) * named * (1.0 - aff)
            return carry

        lax.fori_loop(0, NB, body, 0, unroll=8)

    def router_product():
        rest = lg[...].reshape(T, E)
        acc = None
        for _ in range(3):
            top = rest.astype(bf16)
            term = dot_nn(tokT[...], top)
            acc = term if acc is None else acc + term
            rest = rest - top.astype(f32)
        out_r[...] = acc

    def rs_copy(d, way, c):
        cut = (d, way - 1, rows_of(c), lanes_of(c))
        return remote(
            rs_src.at[cut], rs_dst.at[cut], rs_s.at[d, c], rs_r.at[d, way - 1, c], zdev(d, way)
        )

    def rs_sent(d, c):
        cut = (d, pl.ds(0, half if c // 2 == d else half - 1), rows_of(c), lanes_of(c))
        return remote(rs_src.at[cut], rs_dst.at[cut], rs_s.at[d, c], rs_r.at[d, 0, c], zdev(d, 1))

    def rs_has(d, way, c):
        return way < half or c // 2 == d

    def cut_of(value, c):
        return value[(c // 2) * CR : (c // 2 + 1) * CR, (c % 2) * S : (c % 2 + 1) * S]

    def rs_step(way):
        ahead = [part(behind(1 - d, way)) for d in range(2)] if way < half else [part(behind(0, half))] * 2
        for cc in range(4):
            for d in range(2):
                c = cc if d == 0 else (cc + 2) % 4
                if not rs_has(d, way, c):
                    continue
                acc = cut_of(ahead[d], c)
                if way < half and way + 1 != JUMP and rs_has(d, way + 1, c):
                    rs_copy(d, way + 1, c).wait_recv()
                    acc = acc + rs_dst[d, way, rows_of(c), lanes_of(c)].astype(f32)
                rs_src[d, way - 1, rows_of(c), lanes_of(c)] = acc.astype(bf16)
                rs_copy(d, way, c).start()

    last = max(JUMP, 1)
    for st, way in enumerate(range(half, last - 1, -1)):
        rs_step(way)
        z_step(st)
        if st == 0:
            x_all(2).wait_recv()
            mix_tokens()
        if 1 <= st < JUMP:
            rs_step(JUMP - st)

    mine = part(n)
    z_step(len(plan) - 1)
    bufG[g, i] = jnp.sum(gz[...], axis=0)
    each(NI, lambda r: gx_copy(r).start())
    for c in range(4):
        acc = cut_of(mine, c)
        for d in range(2):
            for way in sorted({1, last}):
                if rs_has(d, way, c):
                    rs_copy(d, way, c).wait_recv()
                    acc = acc + rs_dst[d, way - 1, rows_of(c), lanes_of(c)].astype(f32)
        finv[rows_of(c), lanes_of(c)] = acc.astype(bf16)
    if FP > FS:
        finv[FS:FP, :] = jnp.zeros((FP - FS, 2 * S), bf16)

    def tx_copy(r):
        return remote(tbuf.at[r], rbuf.at[r], xs.at[4], xr.at[4], peer("inner", r))

    def tx_all():
        cut = pl.ds(1, NI - 1)
        return remote(tbuf.at[cut], rbuf.at[cut], xs.at[4], xr.at[4], peer("inner", 1))

    def ty_copy(r):
        to = lax.rem(g + r, NG)
        return remote(ysrc.at[to], ydst.at[r], ys.at[4], yr.at[4], peer("group", r))

    def ty_all():
        return remote(
            ysrc.at[pl.ds(0, NG - 1)], ydst.at[pl.ds(1, NG - 1)], ys.at[4], yr.at[4], peer("group", 1)
        )

    def token_rows(at):
        return dot_nt(pmix[:, at].reshape(NG * 16, 2 * S), finv[...])

    def send_rows(r):
        tbuf[r] = token_rows(lax.rem(i + r, NI)).astype(bf16).reshape(NG, 16, FP)
        tx_copy(r).start()

    each(NI, send_rows)
    acc = token_rows(i)
    gx_all().wait_recv()
    each(NG, lambda r: gy_copy(r).start())
    tx_all().wait_recv()
    for r in range(1, NI):
        acc = acc + rbuf[r].astype(f32).reshape(NG * 16, FP)
    yacc[...] = acc.reshape(NG, 16, FP)
    ysrc[...] = acc.astype(bf16).reshape(NG, 16, FP)
    each(NG, lambda r: ty_copy(r).start())
    gy_all().wait_recv()
    router_side()
    extra = dot_nt(lg[q], rwv[pl.ds(pl.multiple_of(n * FS, 8), FS), :], precision=HI)
    router_product()
    total = yacc[g]
    ty_all().wait_recv()
    for r in range(1, NG):
        total = total + ydst[r].astype(f32)
    out_x[...] = (total[:, 0:FS] + extra).astype(bf16)

    for t in range(3):
        y_all(t).wait_send()
        x_all(t).wait_send()
    gx_all().wait_send()
    gy_all().wait_send()
    tx_all().wait_send()
    ty_all().wait_send()
    for d in range(2):
        z_sent(d).wait_send()
        for c in range(4):
            ag_sent(d, c).wait_send()
            rs_sent(d, c).wait_send()


def local(
    token_inputs, out_grads, expert_ids, router_weight,
    gate_weight, up_weight, down_weight, saved_gate, saved_up,
):
    NG, NI, NZ = lax.axis_size("group"), lax.axis_size("inner"), lax.axis_size("dp")
    NB = NG * NI
    tokens, D = token_inputs.shape
    E = router_weight.shape[1]
    K = expert_ids.shape[1]
    F = down_weight.shape[1]
    S = saved_gate.shape[1]
    T = NB * tokens
    FS = D // NZ
    FP = -(-(FS + K) // 128) * 128
    half = NZ // 2
    vmem = pl.BlockSpec(memory_space=pltpu.VMEM)
    hbm = pl.BlockSpec(memory_space=pl.ANY)
    V = pltpu.VMEM
    dma = pltpu.SemaphoreType.DMA
    scratch = [
        V((2, F, D), bf16), V((2, F, D), bf16), V((2, F, D), bf16),
        V((2, F, S), bf16), V((2, F, S), bf16), V((D, E), f32), V((NZ, 2 * F, FP), bf16),
        V((NG, NI, 16, FP), bf16), V((NG, NI, 16, FP + E), bf16), V((NG, NI, 16, E), f32),
        V((2 * S, T), bf16), V((NG, NI, 16, 2 * S), bf16), V((D, 4 * F), bf16),
        V((FS, T), bf16), V((NZ, FS, 2 * S), bf16), V((2, 2, F, S), f32),
        V((NZ, 2, S), f32), V((NG, NI, 2, S), f32), V((E, S), f32), V((S, E), f32),
        V((NB, 16, E), f32),
        V((2, half, FS, 2 * S), bf16), V((2, half, FS, 2 * S), bf16), V((FP, 2 * S), bf16),
        V((NI, NG, 16, FP), bf16), V((NI, NG, 16, FP), bf16), V((NG, 16, FP), bf16),
        V((NG, 16, FP), f32), V((NG, 16, FP), bf16),
        dma((6,)), dma((5,)), dma((5,)), dma((5,)), dma((5,)),
        dma((2, 4)), dma((2, half, 4)), dma((2, 4)), dma((2, half, 4)),
        dma((2,)), dma((2, half)),
    ]
    return pl.pallas_call(
        functools.partial(kernel, NZ, NG, NI, K),
        out_shape=(
            jax.ShapeDtypeStruct((tokens, FS), bf16),
            jax.ShapeDtypeStruct((FS, E), f32),
        ),
        in_specs=[vmem] * 3 + [hbm] * 6,
        out_specs=(vmem, vmem),
        scratch_shapes=scratch,
        compiler_params=pltpu.CompilerParams(
            collective_id=0, has_side_effects=True, vmem_limit_bytes=58 * 1024 * 1024
        ),
        name="expert_backward",
    )(
        expert_ids.T, out_grads, token_inputs, router_weight,
        jnp.swapaxes(gate_weight, 1, 2), jnp.swapaxes(up_weight, 1, 2), down_weight,
        jnp.swapaxes(saved_gate, 1, 2), jnp.swapaxes(saved_up, 1, 2),
    )


def solution(mesh):
    placed = (
        P(("group", "inner"), None),
        P(("group", "inner"), None),
        P(("group", "inner"), None),
        P(),
        P(("group", "inner"), None, "dp"),
        P(("group", "inner"), None, "dp"),
        P(("group", "inner"), "dp", None),
        P(("group", "inner"), None, "dp"),
        P(("group", "inner"), None, "dp"),
    )
    return jax.shard_map(
        local,
        mesh=mesh,
        in_specs=placed,
        out_specs=(P(("group", "inner"), "dp"), P("dp", None)),
        check_vma=False,
    )
```

```python
import functools

import jax
import jax.numpy as jnp
from jax import lax
from jax.experimental import pallas as pl
from jax.experimental.pallas import tpu as pltpu
from jax.sharding import PartitionSpec as P

MESH = pl.DeviceIdType.MESH
route_scale = 2.5
f32, bf16 = jnp.float32, jnp.bfloat16
HI = lax.Precision.HIGHEST


def dot_nt(a, b, **kw):
    return lax.dot_general(a, b, (((1,), (1,)), ((), ())), preferred_element_type=f32, **kw)


def dot_nn(a, b):
    return lax.dot_general(a, b, (((1,), (0,)), ((), ())), preferred_element_type=f32)


def iota(shape, dim):
    return lax.broadcasted_iota(jnp.int32, shape, dim)


def kernel(
    NZ, NG, NI, K,
    ids, grads, tok, rw_hbm, gw_hbm, uw_hbm, dw_hbm, sg_hbm, su_hbm,
    out_x, out_r,
    gwv, uwv, dwv, sgv, suv, rwv, dws,
    buf1, buf2, buf3, pt, pmix, wT, tokT, xt, dgu, gz, bufG, gflat, gt, lg,
    rs_src, rs_dst, finv, tbuf, rbuf, ysrc, yacc, ydst,
    load_sem, ys, yr, xs, xr, ag_s, ag_r, rs_s, rs_r, z_s, z_r,
):
    NB = NG * NI
    T = 16 * NB
    S = 2 * NB
    E = 2 * NB
    FP = buf1.shape[3]
    F = dwv.shape[1]
    D = dwv.shape[2]
    FS = D // NZ
    half = NZ // 2
    CR = FS // 2
    JUMP = 3 if half >= 5 else 0
    g, i, n = lax.axis_index("group"), lax.axis_index("inner"), lax.axis_index("dp")
    q = g * NI + i

    load_rw = pltpu.make_async_copy(rw_hbm, rwv, load_sem.at[0])
    loads = [
        pltpu.make_async_copy(dw_hbm, dwv, load_sem.at[1]),
        pltpu.make_async_copy(sg_hbm, sgv, load_sem.at[2]),
        pltpu.make_async_copy(su_hbm, suv, load_sem.at[3]),
    ]
    loads_w = [
        pltpu.make_async_copy(gw_hbm, gwv, load_sem.at[4]),
        pltpu.make_async_copy(uw_hbm, uwv, load_sem.at[5]),
    ]

    def each(count, fn):
        for r in sorted(range(1, count), key=lambda r: -min(r, count - r)):
            fn(r)

    def peer(axis, r):
        me, size = {"group": (g, NG), "inner": (i, NI), "dp": (n, NZ)}[axis]
        return {axis: lax.rem(me + r, size)}

    bar = pltpu.get_barrier_semaphore()
    zpeers = (1, NZ - 1) + ((JUMP, NZ - JUMP) if JUMP else ())
    for axis, offsets in (("dp", zpeers), ("group", range(1, NG)), ("inner", range(1, NI))):
        for r in offsets:
            pl.semaphore_signal(bar, inc=1, device_id=peer(axis, r), device_id_type=MESH)
    load_rw.start()
    for c in loads + loads_w:
        c.start()

    lane_e = iota((16, E), 1).astype(f32)
    eye = (iota((16, 16), 1) == iota((16, 16), 0)).astype(bf16)
    named_ids = dot_nt(eye, ids[...].astype(f32).astype(bf16))
    hits = [named_ids[:, k : k + 1] == lane_e for k in range(K)]
    per_token = jnp.where(hits[0], 1.0, 0.0)
    for k in range(1, K):
        per_token = per_token + jnp.where(hits[k], 1.0, 0.0)
    lower = (iota((16, 16), 1) < iota((16, 16), 0)).astype(bf16)
    earlier = dot_nn(lower, per_token.astype(bf16))
    lane_p = iota((16, FP), 1)
    turn = lax.rem(D - n * FS, D)

    def columns(ref):
        return jnp.where(lane_p < FS, pltpu.roll(ref[...].astype(f32), turn, 1)[:, 0:FP], 0.0)

    rows1 = columns(grads)
    for k in range(K):
        position = jnp.sum(jnp.where(hits[k], earlier, 0.0), axis=1, keepdims=True)
        code = named_ids[:, k : k + 1] + E * position
        rows1 = jnp.where(lane_p == FS + k, code, rows1)
    buf1[g, i] = rows1.astype(bf16)
    buf2[g, i, :, 0:FP] = columns(tok).astype(bf16)
    buf2[g, i, :, FP : FP + E] = (per_token * (1.0 + earlier)).astype(bf16)
    pl.semaphore_wait(bar, NG + NI - 2 + len(zpeers))

    def remote(src, dst, s, r, dev):
        return pltpu.make_async_remote_copy(
            src_ref=src, dst_ref=dst, send_sem=s, recv_sem=r, device_id=dev, device_id_type=MESH
        )

    def y_copy(t, r):
        ref = (buf1, buf2, buf3)[t].at[g, i]
        return remote(ref, ref, ys.at[t], yr.at[t], peer("group", r))

    def y_all(t):
        ref = (buf1, buf2, buf3)[t].at[pl.ds(0, NG - 1), i]
        return remote(ref, ref, ys.at[t], yr.at[t], peer("group", 1))

    def x_copy(t, r):
        buf = (buf1, buf2, buf3)[t]
        return remote(buf.at[:, i], buf.at[:, i], xs.at[t], xr.at[t], peer("inner", r))

    def x_all(t):
        ref = (buf1, buf2, buf3)[t].at[:, pl.ds(0, NI - 1)]
        return remote(ref, ref, xs.at[t], xr.at[t], peer("inner", 1))

    each(NG, lambda r: y_copy(0, r).start())
    each(NG, lambda r: y_copy(1, r).start())
    load_rw.wait()
    parts = 7 if D % (7 * 128) == 0 else half
    cols = D // parts
    scores = None
    for p in range(parts):
        rest = rwv[p * cols : (p + 1) * cols, :]
        left = tok[:, p * cols : (p + 1) * cols]
        for _ in range(3):
            top = rest.astype(bf16)
            term = dot_nn(left, top)
            scores = term if scores is None else scores + term
            rest = rest - top.astype(f32)
    buf3[g, i] = scores
    each(NG, lambda r: y_copy(2, r).start())
    for c in loads:
        c.wait()
    for j in range(2):
        a = sgv[j].astype(f32)
        u = suv[j].astype(f32)
        sig = jax.nn.sigmoid(a)
        dgu[j, 0] = u * sig * (1.0 + a * (1.0 - sig))
        dgu[j, 1] = a * sig

    y_all(0).wait_recv()
    each(NI, lambda r: x_copy(0, r).start())
    down = dwv[...].reshape(2 * F, D)
    for m in range(NZ):
        dws[m, :, 0:FS] = down[:, m * FS : (m + 1) * FS]
    for c in loads_w:
        c.wait()
    for p in range(parts):
        cut = slice(p * cols, (p + 1) * cols)
        rows = jnp.concatenate((gwv[0, :, cut], uwv[0, :, cut], gwv[1, :, cut], uwv[1, :, cut]), axis=0)
        wT[cut, :] = rows.astype(f32).T.astype(bf16)
    x_all(0).wait_recv()

    X = buf1[...].reshape(T, FP)
    sel = (iota((16, FP), 1) == iota((16, FP), 0) + FS).astype(bf16)
    codes = dot_nt(sel, X)
    srow = iota((S, T), 0)
    same = (srow >> 1) == (iota((S, T), 1) >> 4)
    for j in range(2):
        want = (2 * q + j + E * (iota((S, 1), 0) & 1)).astype(f32)
        hit = codes[0:1] == want
        for k in range(1, K):
            hit = hit | (codes[k : k + 1] == want)
        pt[pl.ds(j * S, S), :] = jnp.where(same & hit, 1.0, 0.0).astype(bf16)
    xs_rows = dot_nn(pt[...], X)
    xt[n] = xs_rows.T[0:FS].astype(bf16)

    def rows_of(c):
        return pl.ds((c // 2) * CR, CR)

    def lanes_of(c):
        return pl.ds((c % 2) * S, S)

    def zdev(d, dist):
        by = dist if dist == JUMP else 1
        return {"dp": lax.rem(n + (by if d == 0 else NZ - by), NZ)}

    def behind(d, st):
        return lax.rem(n + (NZ - st if d == 0 else st), NZ)

    def held(d, dist):
        return n if dist == JUMP else behind(d, dist - 1)

    if JUMP:
        chains = [list(range(JUMP, half + 1)), list(range(1, JUMP))]
    else:
        chains = [list(range(1, half + 1))]
    plan = [[(None, ch[0]) for ch in chains]]
    for st in range(1, len(chains[0]) + 1):
        plan.append(
            [(ch[st - 1], ch[st] if st < len(ch) else None) for ch in chains if st <= len(ch)]
        )

    def ag_copy(d, dist, c):
        ref = xt.at[held(d, dist), rows_of(c), lanes_of(c)]
        return remote(ref, ref, ag_s.at[d, c], ag_r.at[d, dist - 1, c], zdev(d, dist))

    def ag_sent(d, c):
        ref = xt.at[pl.ds(0, half if c // 2 == d else half - 1), rows_of(c), lanes_of(c)]
        return remote(ref, ref, ag_s.at[d, c], ag_r.at[d, 0, c], zdev(d, 1))

    def ag_has(d, dist, c):
        return dist < half or c // 2 == d

    def mix_tokens():
        codes_all = buf2[:, :, :, FP : FP + E].reshape(T, E).astype(f32)
        aff = jax.nn.sigmoid(buf3[...].reshape(T, E))
        named = jnp.where(codes_all > 0.0, aff, 0.0)
        mix = (route_scale * named / jnp.sum(named, axis=1, keepdims=True)).astype(bf16)
        owner = (iota((E, 2 * S), 1) >= S).astype(jnp.int32) + 2 * q
        pick = (iota((E, 2 * S), 0) == owner).astype(bf16)
        spread = dot_nn(mix, pick)
        placed = pt[...].astype(f32).T
        pmix[...] = (placed * spread).astype(bf16).reshape(NG, NI, 16, 2 * S)

    def token_transpose():
        rows = buf2[:, :, :, 0:FP].reshape(T, FP)
        tokT[...] = rows.astype(f32).T[0:FS].astype(bf16)

    def hidden_term(m):
        return dot_nn(dws[m, :, 0:FS], xt[m])

    hid = None
    for st, moves in enumerate(plan):
        for came, goes in moves:
            for c in range(4):
                for d in range(2):
                    if came is not None and ag_has(d, came, c):
                        ag_copy(d, came, c).wait_recv()
                    if goes is not None and ag_has(d, goes, c):
                        ag_copy(d, goes, c).start()
        if st == 0:
            y_all(1).wait_recv()
            y_all(2).wait_recv()
            each(NI, lambda r: x_copy(1, r).start())
            each(NI, lambda r: x_copy(2, r).start())
            hid = hidden_term(n)
        for came, goes in moves:
            if came is not None:
                hid = hid + hidden_term(behind(0, came))
                if came < half:
                    hid = hid + hidden_term(behind(1, came))
        if st == len(plan) - 2:
            x_all(1).wait_recv()
            token_transpose()

    both = []
    for j in range(2):
        h = hid[j * F : (j + 1) * F, j * S : (j + 1) * S]
        up = h * dgu[j, 1]
        gz[n, pl.ds(j, 1), :] = jnp.sum(up * suv[j].astype(f32), axis=0, keepdims=True)
        pair = jnp.concatenate((h * dgu[j, 0], up), axis=0).astype(bf16)
        none = jnp.zeros_like(pair)
        both.append(jnp.concatenate((pair, none) if j == 0 else (none, pair), axis=1))
    grads_t = jnp.concatenate(both, axis=0)

    def part(m):
        return dot_nn(wT[pl.ds(pl.multiple_of(m * FS, 16), FS), :], grads_t)

    def z_copy(d, dist):
        ref = gz.at[held(d, dist)]
        return remote(ref, ref, z_s.at[d], z_r.at[d, dist - 1], zdev(d, dist))

    def z_sent(d):
        ref = gz.at[pl.ds(0, half - d)]
        return remote(ref, ref, z_s.at[d], z_r.at[d, 0], zdev(d, 1))

    def z_step(st):
        for came, goes in plan[st]:
            for d in range(2):
                if came is not None and came <= half - d:
                    z_copy(d, came).wait_recv()
                if goes is not None and goes <= half - d:
                    z_copy(d, goes).start()

    def gx_copy(r):
        return remote(bufG.at[g, i], bufG.at[g, i], xs.at[3], xr.at[3], peer("inner", r))

    def gx_all():
        ref = bufG.at[g, pl.ds(0, NI - 1)]
        return remote(ref, ref, xs.at[3], xr.at[3], peer("inner", 1))

    def gy_copy(r):
        return remote(bufG.at[g], bufG.at[g], ys.at[3], yr.at[3], peer("group", r))

    def gy_all():
        ref = bufG.at[pl.ds(0, NG - 1)]
        return remote(ref, ref, ys.at[3], yr.at[3], peer("group", 1))

    def router_side():
        for b in range(NB):
            gflat[2 * b : 2 * b + 2, :] = bufG[b // NI, b % NI]
        gt[...] = gflat[...].T

        def body(b, carry):
            gb, ib = b // NI, lax.rem(b, NI)
            code = buf2[gb, ib, :, FP : FP + E].astype(f32)
            aff = jax.nn.sigmoid(buf3[gb, ib])
            g0 = gt[pl.ds(2 * b, 1), :]
            g1 = gt[pl.ds(2 * b + 1, 1), :]
            grads = jnp.where(code == 1.0, g0, jnp.where(code == 2.0, g1, 0.0))
            named = jnp.where(code > 0.0, aff, 0.0)
            total = jnp.sum(named, axis=1, keepdims=True)
            weighted = jnp.sum(named * grads, axis=1, keepdims=True)
            lg[b] = route_scale * (grads / total - weighted / (total * total)) * named * (1.0 - aff)
            return carry

        lax.fori_loop(0, NB, body, 0, unroll=8)

    def router_product():
        rest = lg[...].reshape(T, E)
        acc = None
        for _ in range(3):
            top = rest.astype(bf16)
            term = dot_nn(tokT[...], top)
            acc = term if acc is None else acc + term
            rest = rest - top.astype(f32)
        out_r[...] = acc

    def rs_copy(d, way, c):
        cut = (d, way - 1, rows_of(c), lanes_of(c))
        return remote(
            rs_src.at[cut], rs_dst.at[cut], rs_s.at[d, c], rs_r.at[d, way - 1, c], zdev(d, way)
        )

    def rs_sent(d, c):
        cut = (d, pl.ds(0, half if c // 2 == d else half - 1), rows_of(c), lanes_of(c))
        return remote(rs_src.at[cut], rs_dst.at[cut], rs_s.at[d, c], rs_r.at[d, 0, c], zdev(d, 1))

    def rs_has(d, way, c):
        return way < half or c // 2 == d

    def cut_of(value, c):
        return value[(c // 2) * CR : (c // 2 + 1) * CR, (c % 2) * S : (c % 2 + 1) * S]

    def rs_step(way):
        ahead = [part(behind(1 - d, way)) for d in range(2)] if way < half else [part(behind(0, half))] * 2
        for cc in range(4):
            for d in range(2):
                c = cc if d == 0 else (cc + 2) % 4
                if not rs_has(d, way, c):
                    continue
                acc = cut_of(ahead[d], c)
                if way < half and way + 1 != JUMP and rs_has(d, way + 1, c):
                    rs_copy(d, way + 1, c).wait_recv()
                    acc = acc + rs_dst[d, way, rows_of(c), lanes_of(c)].astype(f32)
                rs_src[d, way - 1, rows_of(c), lanes_of(c)] = acc.astype(bf16)
                rs_copy(d, way, c).start()

    last = max(JUMP, 1)
    for st, way in enumerate(range(half, last - 1, -1)):
        rs_step(way)
        z_step(st)
        if st == 0:
            x_all(2).wait_recv()
            mix_tokens()
        if 1 <= st < JUMP:
            rs_step(JUMP - st)

    mine = part(n)
    z_step(len(plan) - 1)
    bufG[g, i] = jnp.sum(gz[...], axis=0)
    each(NI, lambda r: gx_copy(r).start())
    for c in range(4):
        acc = cut_of(mine, c)
        for d in range(2):
            for way in sorted({1, last}):
                if rs_has(d, way, c):
                    rs_copy(d, way, c).wait_recv()
                    acc = acc + rs_dst[d, way - 1, rows_of(c), lanes_of(c)].astype(f32)
        finv[rows_of(c), lanes_of(c)] = acc.astype(bf16)
    if FP > FS:
        finv[FS:FP, :] = jnp.zeros((FP - FS, 2 * S), bf16)

    def tx_copy(r):
        return remote(tbuf.at[r], rbuf.at[r], xs.at[4], xr.at[4], peer("inner", r))

    def tx_all():
        cut = pl.ds(1, NI - 1)
        return remote(tbuf.at[cut], rbuf.at[cut], xs.at[4], xr.at[4], peer("inner", 1))

    def ty_copy(r):
        to = lax.rem(g + r, NG)
        return remote(ysrc.at[to], ydst.at[r], ys.at[4], yr.at[4], peer("group", r))

    def ty_all():
        return remote(
            ysrc.at[pl.ds(0, NG - 1)], ydst.at[pl.ds(1, NG - 1)], ys.at[4], yr.at[4], peer("group", 1)
        )

    def token_rows(at):
        return dot_nt(pmix[:, at].reshape(NG * 16, 2 * S), finv[...])

    def send_rows(r):
        tbuf[r] = token_rows(lax.rem(i + r, NI)).astype(bf16).reshape(NG, 16, FP)
        tx_copy(r).start()

    each(NI, send_rows)
    acc = token_rows(i)
    gx_all().wait_recv()
    each(NG, lambda r: gy_copy(r).start())
    tx_all().wait_recv()
    for r in range(1, NI):
        acc = acc + rbuf[r].astype(f32).reshape(NG * 16, FP)
    yacc[...] = acc.reshape(NG, 16, FP)
    ysrc[...] = acc.astype(bf16).reshape(NG, 16, FP)
    each(NG, lambda r: ty_copy(r).start())
    gy_all().wait_recv()
    router_side()
    extra = dot_nt(lg[q], rwv[pl.ds(pl.multiple_of(n * FS, 8), FS), :], precision=HI)
    router_product()
    total = yacc[g]
    ty_all().wait_recv()
    for r in range(1, NG):
        total = total + ydst[r].astype(f32)
    out_x[...] = (total[:, 0:FS] + extra).astype(bf16)

    for t in range(3):
        y_all(t).wait_send()
        x_all(t).wait_send()
    gx_all().wait_send()
    gy_all().wait_send()
    tx_all().wait_send()
    ty_all().wait_send()
    for d in range(2):
        z_sent(d).wait_send()
        for c in range(4):
            ag_sent(d, c).wait_send()
            rs_sent(d, c).wait_send()


def local(
    token_inputs, out_grads, expert_ids, router_weight,
    gate_weight, up_weight, down_weight, saved_gate, saved_up,
):
    NG, NI, NZ = lax.axis_size("group"), lax.axis_size("inner"), lax.axis_size("dp")
    NB = NG * NI
    tokens, D = token_inputs.shape
    E = router_weight.shape[1]
    K = expert_ids.shape[1]
    F = down_weight.shape[1]
    S = saved_gate.shape[1]
    T = NB * tokens
    FS = D // NZ
    FP = -(-(FS + K) // 128) * 128
    half = NZ // 2
    vmem = pl.BlockSpec(memory_space=pltpu.VMEM)
    hbm = pl.BlockSpec(memory_space=pl.ANY)
    V = pltpu.VMEM
    dma = pltpu.SemaphoreType.DMA
    scratch = [
        V((2, F, D), bf16), V((2, F, D), bf16), V((2, F, D), bf16),
        V((2, F, S), bf16), V((2, F, S), bf16), V((D, E), f32), V((NZ, 2 * F, FP), bf16),
        V((NG, NI, 16, FP), bf16), V((NG, NI, 16, FP + E), bf16), V((NG, NI, 16, E), f32),
        V((2 * S, T), bf16), V((NG, NI, 16, 2 * S), bf16), V((D, 4 * F), bf16),
        V((FS, T), bf16), V((NZ, FS, 2 * S), bf16), V((2, 2, F, S), f32),
        V((NZ, 2, S), f32), V((NG, NI, 2, S), f32), V((E, S), f32), V((S, E), f32),
        V((NB, 16, E), f32),
        V((2, half, FS, 2 * S), bf16), V((2, half, FS, 2 * S), bf16), V((FP, 2 * S), bf16),
        V((NI, NG, 16, FP), bf16), V((NI, NG, 16, FP), bf16), V((NG, 16, FP), bf16),
        V((NG, 16, FP), f32), V((NG, 16, FP), bf16),
        dma((6,)), dma((5,)), dma((5,)), dma((5,)), dma((5,)),
        dma((2, 4)), dma((2, half, 4)), dma((2, 4)), dma((2, half, 4)),
        dma((2,)), dma((2, half)),
    ]
    return pl.pallas_call(
        functools.partial(kernel, NZ, NG, NI, K),
        out_shape=(
            jax.ShapeDtypeStruct((tokens, FS), bf16),
            jax.ShapeDtypeStruct((FS, E), f32),
        ),
        in_specs=[vmem] * 3 + [hbm] * 6,
        out_specs=(vmem, vmem),
        scratch_shapes=scratch,
        compiler_params=pltpu.CompilerParams(
            collective_id=0, has_side_effects=True, vmem_limit_bytes=58 * 1024 * 1024
        ),
        name="expert_backward",
    )(
        expert_ids.T, out_grads, token_inputs, router_weight,
        jnp.swapaxes(gate_weight, 1, 2), jnp.swapaxes(up_weight, 1, 2), down_weight,
        jnp.swapaxes(saved_gate, 1, 2), jnp.swapaxes(saved_up, 1, 2),
    )


def solution(mesh):
    placed = (
        P(("group", "inner"), None),
        P(("group", "inner"), None),
        P(("group", "inner"), None),
        P(),
        P(("group", "inner"), None, "dp"),
        P(("group", "inner"), None, "dp"),
        P(("group", "inner"), "dp", None),
        P(("group", "inner"), None, "dp"),
        P(("group", "inner"), None, "dp"),
    )
    return jax.shard_map(
        local,
        mesh=mesh,
        in_specs=placed,
        out_specs=(P(("group", "inner"), "dp"), P("dp", None)),
        check_vma=False,
    )
```
